256 devices in a mesh: grp: 1, blk: 32 (over y, x, core), head: 8 (over z).
Axes of the slice: x: 4, y: 4, z: 8, core: 2. Of those that a mesh axis runs over, the one named last changes fastest.
Arguments:
- answer_probe_vectors: bfloat16 [32, 128, 8192], P(('grp', 'blk'), None, 'head')
- answer_lookup_vectors: bfloat16 [32, 128, 1024], P(('grp', 'blk'), None, 'head'), may hold values from -6 to 6
- answer_content_vectors: bfloat16 [32, 128, 1024], P(('grp', 'blk'), None, 'head'), may hold values from -6 to 6
- common_context_lookups: bfloat16 [16384, 1024], P(('grp', 'blk'), 'head')
- common_context_contents: bfloat16 [16384, 1024], P(('grp', 'blk'), 'head'), may hold values from -6 to 6
- place_answer_number: int32 [32], P('grp'), may hold values from 0 to 31, each once
- answer_token_count: int32 [32], P(('grp', 'blk')), may hold values from 32 to 128, as said below
- passing_answers: int32 [1], P('grp'), may hold values from 8 to 32
Outputs:
- attended: bfloat16 [32, 128, 8192], P(('grp', 'blk'), None, 'head')
The draws below stay inside these ranges and needn't reach their ends.
Inputs may be any that keep to these rules, and one draw needn't show every extreme that they name: `place_answer_number`: each response of the group stands in exactly one slot. `answer_token_count`: some slot holds a response of 128 tokens, some one of 32.
All inputs are finite; a program needn't handle non-finite values.
Results may differ from the reference program's by a relative error of at most 0.01.
Values may be sent and summed in bfloat16 or wider, within the bound.
No kernel may reach another device: no remote copies, remote signals or barrier semaphores. Data moves between devices by JAX's collectives and lax.ppermute only.
A program may use at most 192 MiB of HBM per device.

```python
import jax
import jax.numpy as jnp
from jax import lax

QUERY_HEADS = 64
KEY_VALUE_HEADS = 8
HEAD_WIDTH = 128
SLOT_TOKENS = 128
BATCH_PLACES = 32
PROMPT_LENGTH = 16384


def draw_answer_probe_vectors(key, part):
    array_shape = (BATCH_PLACES, SLOT_TOKENS, QUERY_HEADS * HEAD_WIDTH)
    base_offset = jnp.clip(jax.random.normal(jax.random.fold_in(key, 3), array_shape, jnp.float32), -6.0, 6.0)
    return base_offset.astype(jnp.bfloat16)


def draw_common_context_lookups(key, part):
    array_shape = (PROMPT_LENGTH, KEY_VALUE_HEADS * HEAD_WIDTH)
    base_offset = jnp.clip(jax.random.normal(jax.random.fold_in(key, 4), array_shape, jnp.float32), -6.0, 6.0)
    return base_offset.astype(jnp.bfloat16)


def draw_answer_token_count(key, part):
    base_offset = jax.random.randint(jax.random.fold_in(key, 1), (BATCH_PLACES,), SLOT_TOKENS // 4, SLOT_TOKENS + 1)
    slot_order = jax.random.permutation(jax.random.fold_in(key, 2), BATCH_PLACES)
    base_offset = base_offset.at[slot_order[0]].set(SLOT_TOKENS)
    base_offset = base_offset.at[slot_order[1]].set(SLOT_TOKENS // 4)
    return base_offset.astype(jnp.int32)


def shard_levels(own_key, shape, pieces, smallest, high):
    loudness = 1.0
    for position, blocks in pieces:
        draws = jax.random.uniform(jax.random.fold_in(jax.random.fold_in(own_key, 6), position), (blocks,), jnp.float32, smallest / len(pieces), high / len(pieces))
        loudness = loudness * jnp.repeat(jnp.exp(draws), shape[position] // blocks).reshape((-1,) + (1,) * (len(shape) - 1 - position))
    return loudness


def scatter_about(stream_key, shape, spread, reach, shards=(), kind=jnp.bfloat16):
    entries = spread * jax.random.normal(stream_key, shape, jnp.float32)
    if shards:
        entries = entries * shard_levels(stream_key, shape, shards, -0.22, 0.18)
    return jnp.clip(entries, -reach, reach).astype(kind)


def setup_inputs(seed: int = 0, part: int = 0) -> dict:
    keys = jax.random.split(jax.random.key(seed), 9)
    part_keys = jax.random.split(jax.random.fold_in(keys[8], part), 9)
    answer_probe_vectors = draw_answer_probe_vectors(jax.random.fold_in(jax.random.fold_in(keys[8], part), 71), part)
    answer_lookup_vectors = scatter_about(part_keys[1], (BATCH_PLACES, SLOT_TOKENS, KEY_VALUE_HEADS * HEAD_WIDTH), 1.0, 6.0, ((0, 32), (2, 8)))
    answer_content_vectors = scatter_about(part_keys[2], (BATCH_PLACES, SLOT_TOKENS, KEY_VALUE_HEADS * HEAD_WIDTH), 1.0, 6.0, ((0, 32), (2, 8)))
    common_context_lookups = draw_common_context_lookups(jax.random.fold_in(jax.random.fold_in(keys[8], part), 71), part)
    common_context_contents = scatter_about(part_keys[4], (PROMPT_LENGTH, KEY_VALUE_HEADS * HEAD_WIDTH), 1.0, 6.0, ((0, 32), (1, 8)))
    place_answer_number = jax.random.permutation(part_keys[5], BATCH_PLACES).astype(jnp.int32)
    answer_token_count = draw_answer_token_count(jax.random.fold_in(jax.random.fold_in(keys[8], part), 71), part)
    passing_answers = jax.random.randint(part_keys[7], (1,), BATCH_PLACES // 4, BATCH_PLACES + 1).astype(jnp.int32)
    return dict(answer_probe_vectors=answer_probe_vectors, answer_lookup_vectors=answer_lookup_vectors, answer_content_vectors=answer_content_vectors, common_context_lookups=common_context_lookups, common_context_contents=common_context_contents, place_answer_number=place_answer_number, answer_token_count=answer_token_count, passing_answers=passing_answers)


def reference(answer_probe_vectors, answer_lookup_vectors, answer_content_vectors, common_context_lookups, common_context_contents, place_answer_number, answer_token_count, passing_answers):
    group_members = QUERY_HEADS // KEY_VALUE_HEADS
    scale = 1.0 / (HEAD_WIDTH ** 0.5)
    joined_keys = common_context_lookups.astype(jnp.float32).reshape(PROMPT_LENGTH, KEY_VALUE_HEADS, HEAD_WIDTH)
    joined_values = common_context_contents.astype(jnp.float32).reshape(PROMPT_LENGTH, KEY_VALUE_HEADS, HEAD_WIDTH)
    positions = jnp.arange(SLOT_TOKENS, dtype=jnp.int32)
    place_occupied = place_answer_number < passing_answers[0]

    def one_slot(operands):
        query_rows, key_rows, value_rows, length, living = operands
        flat_queries = query_rows.astype(jnp.float32).reshape(SLOT_TOKENS, KEY_VALUE_HEADS, group_members, HEAD_WIDTH)
        flat_keys = key_rows.astype(jnp.float32).reshape(SLOT_TOKENS, KEY_VALUE_HEADS, HEAD_WIDTH)
        flat_values = value_rows.astype(jnp.float32).reshape(SLOT_TOKENS, KEY_VALUE_HEADS, HEAD_WIDTH)
        prompt_scores = jnp.einsum('tkgd,jkd->tkgj', flat_queries, joined_keys) * scale
        own_scores = jnp.einsum('tkgd,ukd->tkgu', flat_queries, flat_keys) * scale
        allowed = (positions[None, :] <= positions[:, None]) & (positions[None, :] < length)
        own_scores = jnp.where(allowed[:, None, None, :], own_scores, jnp.float32(-1e30))
        peak = jnp.maximum(prompt_scores.max(-1), own_scores.max(-1))
        prompt_exp = jnp.exp(prompt_scores - peak[..., None])
        own_exp = jnp.where(allowed[:, None, None, :], jnp.exp(own_scores - peak[..., None]), jnp.float32(0.0))
        total = prompt_exp.sum(-1) + own_exp.sum(-1)
        prompt_w = prompt_exp.astype(jnp.bfloat16).astype(jnp.float32)
        own_w = own_exp.astype(jnp.bfloat16).astype(jnp.float32)
        numer = jnp.einsum('tkgj,jkd->tkgd', prompt_w, joined_values) + jnp.einsum('tkgu,ukd->tkgd', own_w, flat_values)
        result = numer / total[..., None]
        keep = (positions < length) & living
        result = jnp.where(keep[:, None, None, None], result, jnp.float32(0.0))
        return result.reshape(SLOT_TOKENS, QUERY_HEADS * HEAD_WIDTH).astype(jnp.bfloat16)

    return lax.map(one_slot, (answer_probe_vectors, answer_lookup_vectors, answer_content_vectors, answer_token_count, place_occupied))
```

```python
import functools

import jax
import jax.numpy as jnp
import numpy as np
from jax import lax
from jax.experimental import pallas as pl
from jax.experimental.pallas import tpu as pltpu
from jax.sharding import PartitionSpec as P

WIDTH = 128
HEADS = 8
TOKENS = 128
STEP = 32
SCALE = float(np.log2(np.e) / np.sqrt(WIDTH))
ROWS, COLS = 4, 4
F32, BF16 = jnp.float32, jnp.bfloat16


def place(y, x, c):
    return (y % ROWS * COLS + x % COLS) * 2 + c % 2


def shifted(block, dy, dx, dc):
    route = [
        (place(y, x, c), place(y + dy, x + dx, c + dc))
        for y in range(ROWS)
        for x in range(COLS)
        for c in range(2)
    ]
    return lax.ppermute(block, "blk", route)


def dot_t(a, b):
    return lax.dot_general(a, b, (((1,), (1,)), ((), ())), preferred_element_type=F32)


def dot(a, b):
    return lax.dot_general(a, b, (((1,), (0,)), ((), ())), preferred_element_type=F32)


def lane_max(s):
    best = s[:, :128]
    for j in range(1, s.shape[1] // 128):
        best = jnp.maximum(best, s[:, j * 128 : (j + 1) * 128])
    return jnp.max(best, 1, keepdims=True)


def split_scaled(q):
    full = q.astype(F32) * SCALE
    high = full.astype(BF16)
    low = (full - high.astype(F32)).astype(BF16)
    return jnp.concatenate([high, low], 1)


def twice(k):
    return jnp.concatenate([k, k], 1)


def with_ones(v):
    return jnp.concatenate([v, jnp.ones_like(v)], 1)


def count_of(q_ref):
    return jnp.max(q_ref[TOKENS:, :WIDTH].astype(F32)).astype(jnp.int32)


def prompt_kernel(own, n_kv, *refs):
    refs = list(refs)
    q_ref = refs.pop(0)
    kv_refs = [refs.pop(0) for _ in range(n_kv)]
    own_k_ref, own_v_ref = (refs.pop(0), refs.pop(0)) if own else (None, None)
    o_ref = refs.pop(0)
    lane = lax.broadcasted_iota(jnp.int32, (STEP, WIDTH), 1)
    count = count_of(q_ref)
    keys = kv_refs[0].shape[0] // 2

    def block(i, carry):
        row = pl.multiple_of(i * STEP, STEP)
        q = jnp.concatenate(
            [q_ref[pl.ds(row, STEP), h * WIDTH : (h + 1) * WIDTH] for h in range(HEADS)], 0
        )
        q = split_scaled(q)
        peak = total = None
        if own:
            shape = (STEP * HEADS, TOKENS)
            token = row + lax.rem(lax.broadcasted_iota(jnp.int32, shape, 0), STEP)
            u = lax.broadcasted_iota(jnp.int32, shape, 1)
            allowed = (u <= token) & (u < count)
            s = jnp.where(allowed, dot_t(q, twice(own_k_ref[...])), F32(-1e30))
            peak = jnp.max(s, 1, keepdims=True)
            e = jnp.where(allowed, jnp.exp2(s - peak), F32(0.0))
            total = dot(e.astype(BF16), with_ones(own_v_ref[...]))
        for ref in kv_refs:
            s = dot_t(q, twice(ref[:keys, :]))
            top = lane_max(s)
            if peak is not None:
                top = jnp.maximum(peak, top)
            e = jnp.exp2(s - top).astype(BF16)
            added = dot(e, with_ones(ref[keys:, :]))
            total = added if peak is None else total * jnp.exp2(peak - top) + added
            peak = top
        out = (total[:, :WIDTH] / total[:, WIDTH:]).astype(BF16)
        lse = peak + jnp.log2(total[:, WIDTH:])
        stats = jnp.zeros((STEP, WIDTH), F32)
        for h in range(HEADS):
            rows = slice(h * STEP, (h + 1) * STEP)
            o_ref[pl.ds(row, STEP), h * WIDTH : (h + 1) * WIDTH] = out[rows]
            one = lse[rows]
            for part in range(3):
                kept = one.astype(BF16).astype(F32)
                stats = jnp.where(lane == part * HEADS + h, kept, stats)
                one = one - kept
        o_ref[pl.ds(row, STEP), HEADS * WIDTH :] = stats.astype(BF16)
        return carry

    lax.fori_loop(0, (count + (STEP - 1)) // STEP, block, 0)


def merge_kernel(n, q_ref, *refs):
    part_refs, o_ref = refs[:n], refs[n]
    count = count_of(q_ref)
    token = lax.broadcasted_iota(jnp.int32, (STEP, WIDTH), 0)

    def block(i, carry):
        row = pl.multiple_of(i * STEP, STEP)
        at = pl.ds(row, STEP)
        keep = (token + row) < count
        lses = []
        for ref in part_refs:
            stats = ref[at, HEADS * WIDTH :].astype(F32)
            lses.append(
                stats
                + pltpu.roll(stats, WIDTH - HEADS, 1)
                + pltpu.roll(stats, WIDTH - 2 * HEADS, 1)
            )
        peak = functools.reduce(jnp.maximum, lses)
        weights = [jnp.exp2(v - peak) for v in lses]
        inverse = 1.0 / sum(weights)
        weights = [w * inverse for w in weights]
        for h in range(HEADS):
            cols = slice(h * WIDTH, (h + 1) * WIDTH)
            out = sum(
                ref[at, cols].astype(F32) * w[:, h : h + 1]
                for ref, w in zip(part_refs, weights, strict=True)
            )
            o_ref[at, cols] = jnp.where(keep, out, F32(0.0)).astype(BF16)
        return carry

    lax.fori_loop(0, TOKENS // STEP, block, 0)


VMEM = pl.BlockSpec(memory_space=pltpu.VMEM)
PARAMS = pltpu.CompilerParams(vmem_limit_bytes=40 << 20)


def over_prompt(q, kvs, own=()):
    keys = sum(kv.shape[0] // 2 for kv in kvs)
    work = TOKENS * HEADS * keys
    return pl.pallas_call(
        functools.partial(prompt_kernel, bool(own), len(kvs)),
        out_shape=jax.ShapeDtypeStruct((TOKENS, (HEADS + 1) * WIDTH), BF16),
        in_specs=[VMEM] * (1 + len(kvs) + len(own)),
        out_specs=VMEM,
        compiler_params=PARAMS,
        cost_estimate=pl.CostEstimate(
            flops=work * WIDTH * 8, bytes_accessed=2 << 20, transcendentals=work
        ),
        name="over_prompt",
    )(q, *kvs, *own)


def merge(q, parts):
    return pl.pallas_call(
        functools.partial(merge_kernel, len(parts)),
        out_shape=jax.ShapeDtypeStruct((TOKENS, HEADS * WIDTH), BF16),
        in_specs=[VMEM] * (1 + len(parts)),
        out_specs=VMEM,
        compiler_params=PARAMS,
        name="merge",
    )(q, *parts)


def shards(
    answer_probe_vectors,
    answer_lookup_vectors,
    answer_content_vectors,
    common_context_lookups,
    common_context_contents,
    place_answer_number,
    answer_token_count,
    passing_answers,
):
    here = lax.axis_index("blk")
    passing = lax.dynamic_slice_in_dim(place_answer_number, here, 1) < passing_answers
    count = jnp.where(passing, answer_token_count, 0).astype(BF16)
    kv = jnp.concatenate([common_context_lookups, common_context_contents], 0)
    q = jnp.concatenate(
        [answer_probe_vectors[0], jnp.broadcast_to(count[:, None], (16, HEADS * WIDTH))], 0
    )
    qs, kvs = {0: q}, {(0, 0): kv}
    kvs[0, 1] = shifted(kv, 0, 0, 1)
    for d in (1, 3, 2):
        kvs[d, 0] = shifted(kv, 0, d, 0)
        qs[d] = shifted(q, d, 0, 0)
    for d in (1, 3, 2):
        kvs[d, 1] = shifted(kvs[d, 0], 0, 0, 1)
    kv_list = list(kvs.values())
    parts = []
    for d in (2, 1, 3):
        part = over_prompt(qs[d], kv_list)
        parts.append(shifted(part, -d, 0, 0))
    parts.append(
        over_prompt(q, kv_list, (answer_lookup_vectors[0], answer_content_vectors[0]))
    )
    return merge(q, parts)[None]


def solution(mesh):
    placed = (
        P(("grp", "blk"), None, "head"),
        P(("grp", "blk"), None, "head"),
        P(("grp", "blk"), None, "head"),
        P(("grp", "blk"), "head"),
        P(("grp", "blk"), "head"),
        P("grp"),
        P(("grp", "blk")),
        P("grp"),
    )
    return jax.shard_map(
        shards,
        mesh=mesh,
        in_specs=placed,
        out_specs=P(("grp", "blk"), None, "head"),
        check_vma=False,
    )
```

```python
import functools

import jax
import jax.numpy as jnp
import numpy as np
from jax import lax
from jax.experimental import pallas as pl
from jax.experimental.pallas import tpu as pltpu
from jax.sharding import PartitionSpec as P

WIDTH = 128
HEADS = 8
TOKENS = 128
PIECE = 512
STEP = 32
SCALE = float(np.log2(np.e) / np.sqrt(WIDTH))
ROWS, COLS = 4, 4
F32, BF16 = jnp.float32, jnp.bfloat16


def place(y, x, c):
    return (y * COLS + x) * 2 + c


def swapped(block, y_bits, x_bits, c_bits):
    route = [
        (place(y, x, c), place(y ^ y_bits, x ^ x_bits, c ^ c_bits))
        for y in range(ROWS)
        for x in range(COLS)
        for c in range(2)
    ]
    return lax.ppermute(block, "blk", route)


def dot_t(a, b):
    return lax.dot_general(a, b, (((1,), (1,)), ((), ())), preferred_element_type=F32)


def dot(a, b):
    return lax.dot_general(a, b, (((1,), (0,)), ((), ())), preferred_element_type=F32)


def lane_max(s):
    best = s[:, :128]
    for j in range(1, s.shape[1] // 128):
        best = jnp.maximum(best, s[:, j * 128 : (j + 1) * 128])
    return jnp.max(best, 1, keepdims=True)


def split_scaled(q):
    full = q.astype(F32) * SCALE
    high = full.astype(BF16)
    low = (full - high.astype(F32)).astype(BF16)
    return jnp.concatenate([high, low], 1)


def twice(k):
    return jnp.concatenate([k, k], 1)


def with_ones(v):
    return jnp.concatenate([v, jnp.ones_like(v)], 1)


def kept_tokens(q_ref):
    return jnp.max(q_ref[TOKENS:, :WIDTH].astype(F32)).astype(jnp.int32)


def rows_of(q_ref, row, tokens):
    return jnp.concatenate(
        [q_ref[pl.ds(row, tokens), h * WIDTH : (h + 1) * WIDTH] for h in range(HEADS)], 0
    )


def steps_of(q_ref):
    return (kept_tokens(q_ref) + (STEP - 1)) // STEP


def far_kernel(n_kv, q_ref, q_far_ref, *refs):
    kv_refs, own_refs, (o_far_ref, o_own_ref) = refs[:n_kv], refs[n_kv : n_kv + 2], refs[n_kv + 2 :]
    mine, far = steps_of(q_ref), steps_of(q_far_ref)
    slot_over_prompt(q_far_ref, kv_refs, (), o_far_ref, 0, far)
    slot_over_prompt(q_ref, kv_refs, own_refs, o_own_ref, 0, jnp.maximum(mine - far, 0))


def near_kernel(n_kv, q_ref, q_far_ref, q_a_ref, q_b_ref, *refs):
    kv_refs, own_refs, refs = refs[:n_kv], refs[n_kv : n_kv + 2], refs[n_kv + 2 :]
    old_own_ref, o_a_ref, o_b_ref, o_own_ref = refs
    o_own_ref[...] = old_own_ref[...]
    mine, far, near_a, near_b = map(steps_of, (q_ref, q_far_ref, q_a_ref, q_b_ref))
    least = jnp.minimum(jnp.minimum(mine, far), jnp.minimum(near_a, near_b))
    slot_over_prompt(q_a_ref, kv_refs, (), o_a_ref, 0, near_a)
    slot_over_prompt(q_b_ref, kv_refs, (), o_b_ref, 0, near_b)
    slot_over_prompt(q_ref, kv_refs, own_refs, o_own_ref, jnp.maximum(mine - far, 0), mine - least)


def own_kernel(n_kv, q_ref, q_far_ref, q_a_ref, q_b_ref, *refs):
    kv_refs, own_refs, (old_own_ref, o_own_ref) = refs[:n_kv], refs[n_kv : n_kv + 2], refs[n_kv + 2 :]
    o_own_ref[...] = old_own_ref[...]
    mine, far, near_a, near_b = map(steps_of, (q_ref, q_far_ref, q_a_ref, q_b_ref))
    least = jnp.minimum(jnp.minimum(mine, far), jnp.minimum(near_a, near_b))
    slot_over_prompt(q_ref, kv_refs, own_refs, o_own_ref, mine - least, mine)


def slot_over_prompt(q_ref, kv_refs, own_refs, o_ref, begin, end):
    count = kept_tokens(q_ref)

    def block(row, tokens):
        rows = tokens * HEADS
        q = split_scaled(rows_of(q_ref, row, tokens))
        peak = total = None
        if own_refs:
            own_k_ref, own_v_ref = own_refs
            shape = (rows, TOKENS)
            token = row + (lax.broadcasted_iota(jnp.int32, shape, 0) & (tokens - 1))
            u = lax.broadcasted_iota(jnp.int32, shape, 1)
            allowed = (u <= token) & (u < count)
            s = jnp.where(allowed, dot_t(q, twice(own_k_ref[...])), F32(-1e30))
            peak = jnp.max(s, 1, keepdims=True)
            e = jnp.where(allowed, jnp.exp2(s - peak), F32(0.0))
            total = dot(e.astype(BF16), with_ones(own_v_ref[...]))
        parts = [
            (ref, start) for ref in kv_refs for start in range(0, ref.shape[0], 2 * PIECE)
        ]

        def scores(n):
            ref, start = parts[n]
            return dot_t(q, twice(ref[start : start + PIECE, :]))

        following = scores(0)
        for n, (ref, start) in enumerate(parts):
            s = following
            if n + 1 < len(parts):
                following = scores(n + 1)
            top = lane_max(s)
            if peak is not None:
                top = jnp.maximum(peak, top)
            e = jnp.exp2(s - top).astype(BF16)
            added = dot(e, with_ones(ref[start + PIECE : start + 2 * PIECE, :]))
            total = added if peak is None else total * jnp.exp2(peak - top) + added
            peak = top
        lane = lax.broadcasted_iota(jnp.int32, (tokens, WIDTH), 1)
        packed_sum = packed_peak = jnp.zeros((tokens, WIDTH), F32)
        sums = total[:, WIDTH:]
        out = (total[:, :WIDTH] / sums).astype(BF16)
        for h in range(HEADS):
            mine, at = (lane & (HEADS - 1)) == h, slice(h * tokens, (h + 1) * tokens)
            o_ref[pl.ds(row, tokens), h * WIDTH : (h + 1) * WIDTH] = out[at]
            packed_sum = jnp.where(mine, sums[at], packed_sum)
            packed_peak = jnp.where(mine, peak[at], packed_peak)
        lse = packed_peak + jnp.log2(packed_sum)
        high = lse.astype(BF16).astype(F32)
        middle = (lse - high).astype(BF16).astype(F32)
        low = lse - high - middle
        stats = jnp.where(lane < HEADS, high, jnp.where(lane < 2 * HEADS, middle, low))
        o_ref[pl.ds(row, tokens), HEADS * WIDTH :] = stats.astype(BF16)

    def pair(i, carry):
        block(pl.multiple_of((begin + 2 * i) * STEP, STEP), 2 * STEP)
        return carry

    lax.fori_loop(0, (end - begin) // 2, pair, 0)

    @pl.when((end - begin) % 2 == 1)
    def _():
        block(pl.multiple_of((end - 1) * STEP, STEP), STEP)


def merge_kernel(n, q_ref, *refs):
    part_refs, o_ref = refs[:n], refs[n]
    count = kept_tokens(q_ref)
    keep = lax.broadcasted_iota(jnp.int32, (TOKENS, WIDTH), 0) < count
    lses = []
    for ref in part_refs:
        stats = ref[:, HEADS * WIDTH :].astype(F32)
        lses.append(
            stats
            + pltpu.roll(stats, WIDTH - HEADS, 1)
            + pltpu.roll(stats, WIDTH - 2 * HEADS, 1)
        )
    peak = functools.reduce(jnp.maximum, lses)
    weights = [jnp.exp2(v - peak) for v in lses]
    inverse = 1.0 / sum(weights)
    weights = [w * inverse for w in weights]
    for h in range(HEADS):
        cols = slice(h * WIDTH, (h + 1) * WIDTH)
        out = sum(
            ref[:, cols].astype(F32) * w[:, h : h + 1]
            for ref, w in zip(part_refs, weights, strict=True)
        )
        o_ref[:, cols] = jnp.where(keep, out, F32(0.0)).astype(BF16)


VMEM = pl.BlockSpec(memory_space=pltpu.VMEM)
PARAMS = pltpu.CompilerParams(vmem_limit_bytes=40 << 20)


def over_prompt(kernel, n_out, qs, kvs, own, *more):
    work = n_out * TOKENS * HEADS * sum(kv.shape[0] // 2 for kv in kvs)
    return pl.pallas_call(
        functools.partial(kernel, len(kvs)),
        out_shape=[jax.ShapeDtypeStruct((TOKENS, (HEADS + 1) * WIDTH), BF16)] * n_out,
        in_specs=[VMEM] * (len(qs) + len(kvs) + len(own) + len(more)),
        out_specs=[VMEM] * n_out,
        compiler_params=PARAMS,
        cost_estimate=pl.CostEstimate(
            flops=work * WIDTH * 8, bytes_accessed=2 << 20, transcendentals=work
        ),
        name="over_prompt",
    )(*qs, *kvs, *own, *more)


def merge(q, parts):
    return pl.pallas_call(
        functools.partial(merge_kernel, len(parts)),
        out_shape=jax.ShapeDtypeStruct((TOKENS, HEADS * WIDTH), BF16),
        in_specs=[VMEM] * (1 + len(parts)),
        out_specs=VMEM,
        compiler_params=PARAMS,
        name="merge",
    )(q, *parts)


def shards(
    answer_probe_vectors,
    answer_lookup_vectors,
    answer_content_vectors,
    common_context_lookups,
    common_context_contents,
    place_answer_number,
    answer_token_count,
    passing_answers,
):
    mine = jnp.arange(place_answer_number.shape[0]) == lax.axis_index("blk")
    kept = mine & (place_answer_number < passing_answers)
    count = jnp.where(kept, answer_token_count, 0).astype(BF16)
    count = jnp.pad(count, (0, HEADS * WIDTH - count.shape[0]))
    q = jnp.concatenate([answer_probe_vectors[0], jnp.broadcast_to(count, (16, count.shape[0]))], 0)
    kv = jnp.concatenate([common_context_lookups, common_context_contents], 0)
    qs, kvs = {0: q}, {(0, 0): kv}
    for bits in (2, 1, 3):
        qs[bits] = swapped(q, bits, 0, 0)
        kvs[bits, 0] = swapped(kv, 0, bits, 0)
    for bits in (0, 1, 3, 2):
        kvs[bits, 1] = swapped(kvs[bits, 0], 0, 0, 1)
    every = list(kvs.values())
    own = (answer_lookup_vectors[0], answer_content_vectors[0])
    part_far, part_own = over_prompt(far_kernel, 2, [q, qs[2]], every, own)
    all_q = [q, qs[2], qs[1], qs[3]]
    part_a, part_b, part_own = over_prompt(near_kernel, 3, all_q, every, own, part_own)
    (part_own,) = over_prompt(own_kernel, 1, all_q, every, own, part_own)
    parts = [swapped(part_far, 2, 0, 0), swapped(part_a, 1, 0, 0), swapped(part_b, 3, 0, 0)]
    return merge(q, [part_own, *parts])[None]


def solution(mesh):
    placed = (
        P(("grp", "blk"), None, "head"),
        P(("grp", "blk"), None, "head"),
        P(("grp", "blk"), None, "head"),
        P(("grp", "blk"), "head"),
        P(("grp", "blk"), "head"),
        P("grp"),
        P(("grp", "blk")),
        P("grp"),
    )
    return jax.shard_map(
        shards,
        mesh=mesh,
        in_specs=placed,
        out_specs=P(("grp", "blk"), None, "head"),
        check_vma=False,
    )
```

```python
import functools

import jax
import jax.numpy as jnp
import numpy as np
from jax import lax
from jax.experimental import pallas as pl
from jax.experimental.pallas import tpu as pltpu
from jax.sharding import PartitionSpec as P

WIDTH = 128
HEADS = 8
TOKENS = 128
PIECE = 512
STEP = 32
SCALE = float(np.log2(np.e) / np.sqrt(WIDTH))
ROWS, COLS = 4, 4
F32, BF16 = jnp.float32, jnp.bfloat16


def place(y, x, c):
    return (y * COLS + x) * 2 + c


def swapped(block, y_bits, x_bits, c_bits):
    route = [
        (place(y, x, c), place(y ^ y_bits, x ^ x_bits, c ^ c_bits))
        for y in range(ROWS)
        for x in range(COLS)
        for c in range(2)
    ]
    return lax.ppermute(block, "blk", route)


def dot_t(a, b):
    return lax.dot_general(a, b, (((1,), (1,)), ((), ())), preferred_element_type=F32)


def dot(a, b):
    return lax.dot_general(a, b, (((1,), (0,)), ((), ())), preferred_element_type=F32)


def lane_max(s):
    best = s[:, :128]
    for j in range(1, s.shape[1] // 128):
        best = jnp.maximum(best, s[:, j * 128 : (j + 1) * 128])
    return jnp.max(best, 1, keepdims=True)


def split_scaled(q):
    full = q.astype(F32) * SCALE
    high = full.astype(BF16)
    low = (full - high.astype(F32)).astype(BF16)
    return jnp.concatenate([high, low], 1)


def twice(k):
    return jnp.concatenate([k, k], 1)


def with_ones(v):
    return jnp.concatenate([v, jnp.ones_like(v)], 1)


def kept_tokens(q_ref):
    return jnp.max(q_ref[TOKENS:, :WIDTH].astype(F32)).astype(jnp.int32)


def rows_of(q_ref, row, tokens):
    return jnp.concatenate(
        [q_ref[pl.ds(row, tokens), h * WIDTH : (h + 1) * WIDTH] for h in range(HEADS)], 0
    )


def steps_of(q_ref):
    return (kept_tokens(q_ref) + (STEP - 1)) // STEP


def far_kernel(n_kv, q_ref, q_far_ref, *refs):
    kv_refs, own_refs, (o_far_ref, o_own_ref) = refs[:n_kv], refs[n_kv : n_kv + 2], refs[n_kv + 2 :]
    mine, far = steps_of(q_ref), steps_of(q_far_ref)
    slot_over_prompt(q_far_ref, kv_refs, (), o_far_ref, 0, far)
    slot_over_prompt(q_ref, kv_refs, own_refs, o_own_ref, 0, jnp.maximum(mine - far, 0))


def near_kernel(n_kv, q_ref, q_far_ref, q_a_ref, q_b_ref, *refs):
    kv_refs, own_refs, refs = refs[:n_kv], refs[n_kv : n_kv + 2], refs[n_kv + 2 :]
    old_own_ref, o_a_ref, o_b_ref, o_own_ref = refs
    o_own_ref[...] = old_own_ref[...]
    mine, far, near_a, near_b = map(steps_of, (q_ref, q_far_ref, q_a_ref, q_b_ref))
    least = jnp.minimum(jnp.minimum(mine, far), jnp.minimum(near_a, near_b))
    slot_over_prompt(q_a_ref, kv_refs, (), o_a_ref, 0, near_a)
    slot_over_prompt(q_b_ref, kv_refs, (), o_b_ref, 0, near_b)
    slot_over_prompt(q_ref, kv_refs, own_refs, o_own_ref, jnp.maximum(mine - far, 0), mine - least)


def own_kernel(n_kv, q_ref, q_far_ref, q_a_ref, q_b_ref, *refs):
    kv_refs, own_refs, (old_own_ref, o_own_ref) = refs[:n_kv], refs[n_kv : n_kv + 2], refs[n_kv + 2 :]
    o_own_ref[...] = old_own_ref[...]
    mine, far, near_a, near_b = map(steps_of, (q_ref, q_far_ref, q_a_ref, q_b_ref))
    least = jnp.minimum(jnp.minimum(mine, far), jnp.minimum(near_a, near_b))
    slot_over_prompt(q_ref, kv_refs, own_refs, o_own_ref, mine - least, mine)


def slot_over_prompt(q_ref, kv_refs, own_refs, o_ref, begin, end):
    count = kept_tokens(q_ref)

    def block(row, tokens):
        rows = tokens * HEADS
        q = split_scaled(rows_of(q_ref, row, tokens))
        peak = total = None
        if own_refs:
            own_k_ref, own_v_ref = own_refs
            shape = (rows, TOKENS)
            token = row + (lax.broadcasted_iota(jnp.int32, shape, 0) & (tokens - 1))
            u = lax.broadcasted_iota(jnp.int32, shape, 1)
            allowed = (u <= token) & (u < count)
            s = jnp.where(allowed, dot_t(q, twice(own_k_ref[...])), F32(-1e30))
            peak = jnp.max(s, 1, keepdims=True)
            e = jnp.where(allowed, jnp.exp2(s - peak), F32(0.0))
            total = dot(e.astype(BF16), with_ones(own_v_ref[...]))
        parts = [
            (ref, start) for ref in kv_refs for start in range(0, ref.shape[0], 2 * PIECE)
        ]

        def scores(n):
            ref, start = parts[n]
            return dot_t(q, twice(ref[start : start + PIECE, :]))

        following = scores(0)
        for n, (ref, start) in enumerate(parts):
            s = following
            if n + 1 < len(parts):
                following = scores(n + 1)
            top = lane_max(s)
            if peak is not None:
                top = jnp.maximum(peak, top)
            e = jnp.exp2(s - top).astype(BF16)
            added = dot(e, with_ones(ref[start + PIECE : start + 2 * PIECE, :]))
            total = added if peak is None else total * jnp.exp2(peak - top) + added
            peak = top
        lane = lax.broadcasted_iota(jnp.int32, (tokens, WIDTH), 1)
        packed_sum = packed_peak = jnp.zeros((tokens, WIDTH), F32)
        sums = total[:, WIDTH:]
        out = (total[:, :WIDTH] / sums).astype(BF16)
        for h in range(HEADS):
            mine, at = (lane & (HEADS - 1)) == h, slice(h * tokens, (h + 1) * tokens)
            o_ref[pl.ds(row, tokens), h * WIDTH : (h + 1) * WIDTH] = out[at]
            packed_sum = jnp.where(mine, sums[at], packed_sum)
            packed_peak = jnp.where(mine, peak[at], packed_peak)
        lse = packed_peak + jnp.log2(packed_sum)
        high = lse.astype(BF16).astype(F32)
        middle = (lse - high).astype(BF16).astype(F32)
        low = lse - high - middle
        stats = jnp.where(lane < HEADS, high, jnp.where(lane < 2 * HEADS, middle, low))
        o_ref[pl.ds(row, tokens), HEADS * WIDTH :] = stats.astype(BF16)

    def pair(i, carry):
        block(pl.multiple_of((begin + 2 * i) * STEP, STEP), 2 * STEP)
        return carry

    lax.fori_loop(0, (end - begin) // 2, pair, 0)

    @pl.when((end - begin) % 2 == 1)
    def _():
        block(pl.multiple_of((end - 1) * STEP, STEP), STEP)


def merge_kernel(n, q_ref, *refs):
    part_refs, (o_ref, held, sems) = refs[:n], refs[n:]
    count = kept_tokens(q_ref)
    half = TOKENS // 2
    copies = []
    for i in range(2):
        at = slice(i * half, (i + 1) * half)
        keep = lax.broadcasted_iota(jnp.int32, (half, WIDTH), 0) + i * half < count
        lses = []
        for ref in part_refs:
            stats = ref[at, HEADS * WIDTH :].astype(F32)
            lses.append(
                stats
                + pltpu.roll(stats, WIDTH - HEADS, 1)
                + pltpu.roll(stats, WIDTH - 2 * HEADS, 1)
            )
        peak = functools.reduce(jnp.maximum, lses)
        weights = [jnp.exp2(v - peak) for v in lses]
        inverse = 1.0 / sum(weights)
        weights = [w * inverse for w in weights]
        for h in range(HEADS):
            cols = slice(h * WIDTH, (h + 1) * WIDTH)
            out = sum(
                ref[at, cols].astype(F32) * w[:, h : h + 1]
                for ref, w in zip(part_refs, weights, strict=True)
            )
            held[at, cols] = jnp.where(keep, out, F32(0.0)).astype(BF16)
        copy = pltpu.make_async_copy(held.at[at, :], o_ref.at[at, :], sems.at[i])
        copy.start()
        copies.append(copy)
    for copy in copies:
        copy.wait()


VMEM = pl.BlockSpec(memory_space=pltpu.VMEM)
PARAMS = pltpu.CompilerParams(vmem_limit_bytes=40 << 20)


def over_prompt(kernel, n_out, qs, kvs, own, *more):
    work = n_out * TOKENS * HEADS * sum(kv.shape[0] // 2 for kv in kvs)
    return pl.pallas_call(
        functools.partial(kernel, len(kvs)),
        out_shape=[jax.ShapeDtypeStruct((TOKENS, (HEADS + 1) * WIDTH), BF16)] * n_out,
        in_specs=[VMEM] * (len(qs) + len(kvs) + len(own) + len(more)),
        out_specs=[VMEM] * n_out,
        compiler_params=PARAMS,
        cost_estimate=pl.CostEstimate(
            flops=work * WIDTH * 8, bytes_accessed=2 << 20, transcendentals=work
        ),
        name="over_prompt",
    )(*qs, *kvs, *own, *more)


def merge(q, parts):
    return pl.pallas_call(
        functools.partial(merge_kernel, len(parts)),
        out_shape=jax.ShapeDtypeStruct((TOKENS, HEADS * WIDTH), BF16),
        in_specs=[VMEM] * (1 + len(parts)),
        out_specs=pl.BlockSpec(memory_space=pl.ANY),
        scratch_shapes=[
            pltpu.VMEM((TOKENS, HEADS * WIDTH), BF16),
            pltpu.SemaphoreType.DMA((2,)),
        ],
        compiler_params=PARAMS,
        name="merge",
    )(q, *parts)


def shards(
    answer_probe_vectors,
    answer_lookup_vectors,
    answer_content_vectors,
    common_context_lookups,
    common_context_contents,
    place_answer_number,
    answer_token_count,
    passing_answers,
):
    mine = jnp.arange(place_answer_number.shape[0]) == lax.axis_index("blk")
    kept = mine & (place_answer_number < passing_answers)
    count = jnp.where(kept, answer_token_count, 0).astype(BF16)
    count = jnp.pad(count, (0, HEADS * WIDTH - count.shape[0]))
    q = jnp.concatenate([answer_probe_vectors[0], jnp.broadcast_to(count, (16, count.shape[0]))], 0)
    kv = jnp.concatenate([common_context_lookups, common_context_contents], 0)
    qs, kvs = {0: q}, {(0, 0): kv}
    for bits in (2, 1, 3):
        qs[bits] = swapped(q, bits, 0, 0)
        kvs[bits, 0] = swapped(kv, 0, bits, 0)
    for bits in (0, 1, 3, 2):
        kvs[bits, 1] = swapped(kvs[bits, 0], 0, 0, 1)
    every = list(kvs.values())
    own = (answer_lookup_vectors[0], answer_content_vectors[0])
    part_far, part_own = over_prompt(far_kernel, 2, [q, qs[2]], every, own)
    all_q = [q, qs[2], qs[1], qs[3]]
    part_a, part_b, part_own = over_prompt(near_kernel, 3, all_q, every, own, part_own)
    (part_own,) = over_prompt(own_kernel, 1, all_q, every, own, part_own)
    parts = [swapped(part_far, 2, 0, 0), swapped(part_a, 1, 0, 0), swapped(part_b, 3, 0, 0)]
    return merge(q, [part_own, *parts])[None]


def solution(mesh):
    placed = (
        P(("grp", "blk"), None, "head"),
        P(("grp", "blk"), None, "head"),
        P(("grp", "blk"), None, "head"),
        P(("grp", "blk"), "head"),
        P(("grp", "blk"), "head"),
        P("grp"),
        P(("grp", "blk")),
        P("grp"),
    )
    return jax.shard_map(
        shards,
        mesh=mesh,
        in_specs=placed,
        out_specs=P(("grp", "blk"), None, "head"),
        check_vma=False,
    )
```
